512 devices in a mesh: dp: 32 (over z, x_lo), mp: 16 (over y, x_hi, core).
Axes of the slice: x: 4 (x_hi: 2, x_lo: 2; x = x_hi * 2 + x_lo), y: 4, z: 16, core: 2. Of those that a mesh axis runs over, the one named last changes fastest.
Arguments:
- tokens: bfloat16 [192, 8192], P(None, ('dp', 'mp')), may hold values from -6 to 6
- out_grad: bfloat16 [192, 8192], P(None, ('dp', 'mp')), may hold values from -6 to 6
- gate_weight: bfloat16 [28672, 8192], P(('dp', 'mp')), may hold values from -0.0625 to 0.0625
- up_weight: bfloat16 [28672, 8192], P(('dp', 'mp')), may hold values from -0.0625 to 0.0625
- down_weight: bfloat16 [28672, 8192], P(('dp', 'mp')), may hold values from -0.03125 to 0.03125
- input_proj: bfloat16 [64, 8192], replicated, may hold values from -0.0625 to 0.0625
- output_proj: bfloat16 [64, 8192], replicated, may hold values from -0.0625 to 0.0625
- gate_proj: bfloat16 [28672, 64], P(('dp', 'mp')), may hold values from -0.03125 to 0.03125
- up_proj: bfloat16 [28672, 64], P(('dp', 'mp')), may hold values from -0.03125 to 0.03125
- hidden_proj: bfloat16 [28672, 64], P(('dp', 'mp')), may hold values from -0.03125 to 0.03125
- doc_ids: int32 [192], replicated, may hold values from 0 to 7, never falling along the last dimension, each value on 1 to 48 neighbouring positions
Outputs:
- doc_grads: float32 [3, 8, 4096], replicated
The draws below stay inside these ranges and needn't reach their ends.
Inputs may be any that keep to these rules, and one draw needn't show every extreme that they name: doc_ids never fall along the tokens; each document has 1 to 48 tokens and one has exactly that many.
All inputs are finite; a program needn't handle non-finite values.
Results may differ from the reference program's by a relative error of at most 0.003.
Values may be sent and summed in bfloat16 or wider, within the bound.
No kernel may reach another device: no remote copies, remote signals or barrier semaphores. Data moves between devices by JAX's collectives and lax.ppermute only.
A program may use at most 64 MiB of HBM per device.

```python
import math
import jax
import jax.numpy as jnp
import numpy as np
from jax import lax

D = 8192
FF = 28672
R = 64
TOKENS = 192
DOCS = 8


def level_of(stream_key, shape, split, low, largest):
    level = 1.0
    for dim, blocks in split:
        heights = jax.random.uniform(jax.random.fold_in(jax.random.fold_in(stream_key, 6), dim), (blocks,), jnp.float32, low / len(split), largest / len(split))
        level = level * jnp.repeat(jnp.exp(heights), shape[dim] // blocks).reshape((-1,) + (1,) * (len(shape) - 1 - dim))
    return level


def length_profile(number_of, total, bound, slope):
    weights = [(1 << 20) // math.isqrt(grade ** slope) + 1 for grade in range(2, number_of + 1)]
    surplus, counts = total - bound - (number_of - 1), [1] * (number_of - 1)
    while surplus > 0:
        candidates = [i for i in range(number_of - 1) if counts[i] < bound]
        pool, remaining = sum([weights[i] for i in candidates]), surplus
        for i in candidates:
            more = min(bound - counts[i], max(1, remaining * weights[i] // pool), surplus)
            counts[i] = counts[i] + more
            surplus = surplus - more
    return np.array([bound] + counts)


def ragged(rng, number_of, total, reach, lean):
    if number_of == 2:
        one = jax.random.randint(rng, (), max(1, total - reach), min(reach, total - 1) + 1)
        return jnp.stack([one, total - one])
    tallies = jnp.asarray(length_profile(number_of, total, reach, lean), jnp.int32)
    pairs = (number_of - 1) // 2
    donor, taker = tallies[1:1 + 2 * pairs:2], tallies[2:2 + 2 * pairs:2]
    slack = jnp.minimum(donor - 1, reach - taker)
    moved = jax.random.randint(jax.random.fold_in(rng, 1), (pairs,), 0, 1 << 20) % (slack + 1)
    tallies = tallies.at[1:1 + 2 * pairs:2].set(donor - moved).at[2:2 + 2 * pairs:2].set(taker + moved)
    return tallies[jax.random.permutation(jax.random.fold_in(rng, 2), number_of)]


def scatter_about(stream_key, shape, scale, bound, split=(), held_as=jnp.bfloat16):
    result = scale * jax.random.normal(stream_key, shape, jnp.float32)
    if split:
        result = result * level_of(stream_key, shape, split, -0.22, 0.18)
    return jnp.clip(result, -bound, bound).astype(held_as)


def setup_inputs(seed: int = 0) -> dict:
    seeds = jax.random.split(jax.random.key(seed), 12)
    tokens = scatter_about(seeds[0], (TOKENS, D), 1.0, 6.0, ((1, 512),))
    out_grad = scatter_about(seeds[1], (TOKENS, D), 1.0, 6.0, ((1, 512),))
    gate_weight = scatter_about(seeds[2], (FF, D), D ** -0.5, 0.0625, ((0, 512),))
    up_weight = scatter_about(seeds[3], (FF, D), D ** -0.5, 0.0625, ((0, 512),))
    down_weight = scatter_about(seeds[4], (FF, D), FF ** -0.5, 0.03125, ((0, 512),))
    input_proj = scatter_about(seeds[5], (R, D), D ** -0.5, 0.0625)
    output_proj = scatter_about(seeds[6], (R, D), D ** -0.5, 0.0625)
    gate_proj = scatter_about(seeds[7], (FF, R), FF ** -0.5, 0.03125, ((0, 512),))
    up_proj = scatter_about(seeds[8], (FF, R), FF ** -0.5, 0.03125, ((0, 512),))
    hidden_proj = scatter_about(seeds[9], (FF, R), FF ** -0.5, 0.03125, ((0, 512),))
    doc_ids = jnp.searchsorted(jnp.cumsum(ragged(seeds[10], DOCS, TOKENS, TOKENS // 4, 1)), jnp.arange(TOKENS), side="right").astype(jnp.int32)
    return {"tokens": tokens, "out_grad": out_grad, "gate_weight": gate_weight, "up_weight": up_weight, "down_weight": down_weight, "input_proj": input_proj, "output_proj": output_proj, "gate_proj": gate_proj, "up_proj": up_proj, "hidden_proj": hidden_proj, "doc_ids": doc_ids}


def outer_docs(left_side, right_side, onehot):
    weighted = (onehot[:, :, None] * left_side[:, None, :]).reshape(left_side.shape[0], -1)
    blocks = jnp.dot(weighted.T, right_side, precision=lax.Precision.HIGHEST, preferred_element_type=jnp.float32)
    return blocks.reshape(onehot.shape[1], -1)


def by_rows(left_side, right_side):
    return lax.dot_general(left_side, right_side, (((1,), (1,)), ((), ())), preferred_element_type=jnp.float32)


def reference(tokens, out_grad, gate_weight, up_weight, down_weight, input_proj, output_proj, gate_proj, up_proj, hidden_proj, doc_ids):
    gate_sum = by_rows(tokens, gate_weight)
    up_sum = by_rows(tokens, up_weight)
    sigmoid_gate = jax.nn.sigmoid(gate_sum)
    silu_gate = gate_sum * sigmoid_gate
    hidden = (silu_gate * up_sum).astype(jnp.bfloat16)
    hidden_grad = by_rows(out_grad, down_weight)
    gate_grad = (hidden_grad * up_sum * sigmoid_gate * (1.0 + gate_sum * (1.0 - sigmoid_gate))).astype(jnp.bfloat16)
    up_grad = (hidden_grad * silu_gate).astype(jnp.bfloat16)
    in_factor = by_rows(tokens, input_proj)
    down_out = by_rows(out_grad, output_proj)
    gate_out = jnp.dot(gate_grad, gate_proj, preferred_element_type=jnp.float32)
    up_out = jnp.dot(up_grad, up_proj, preferred_element_type=jnp.float32)
    down_in = jnp.dot(hidden, hidden_proj, preferred_element_type=jnp.float32)
    onehot = (doc_ids[:, None] == jnp.arange(DOCS, dtype=jnp.int32)[None, :]).astype(jnp.float32)
    return jnp.stack([outer_docs(gate_out, in_factor, onehot), outer_docs(up_out, in_factor, onehot), outer_docs(down_out, down_in, onehot)])
```

```python
import jax
import jax.numpy as jnp
from jax import lax
from jax.experimental import pallas as pl
from jax.experimental.pallas import tpu as pltpu
from jax.sharding import PartitionSpec as P

DOCS = 8
BOTH = ("dp", "mp")
NZ, NXL, NY, NXH, NC = 16, 2, 4, 2, 2
NX = NXL * NXH
PLANE = NX * NY
LOW = 32
HALF = 96
MIB = 1 << 20


def device(z, xl, y, xh, c):
    return (((z * NXL + xl) * NY + y) * NXH + xh) * NC + c


def along_x(z, y, c):
    return [device(z, xl, y, xh, c) for xl in range(NXL) for xh in range(NXH)]


def along_y(z, xl, xh, c):
    return [device(z, xl, y, xh, c) for y in range(NY)]


def x_groups(c):
    return [along_x(z, y, c) for z in range(NZ) for y in range(NY)]


def y_groups(c):
    return [along_y(z, xl, xh, c) for z in range(NZ) for xl in range(NXL) for xh in range(NXH)]


SITES = [(xl, y, xh) for xl in range(NXL) for y in range(NY) for xh in range(NXH)]
COLUMN_GROUPS = [[device(z, *s, c) for z in range(NZ) for c in range(NC)] for s in SITES]
Z_GROUPS = [[device(z, *s, c) for z in range(NZ)] for s in SITES for c in range(NC)]
FIRST_GROUPS = x_groups(0) + y_groups(1)
SECOND_GROUPS = y_groups(0) + x_groups(1)
PLANE_GROUPS = [[device(z, *s, c) for s in SITES] for z in range(NZ) for c in range(NC)]
LAYER_GROUPS = [[device(z, *s, c) for s in SITES for c in range(NC)] for z in range(NZ)]
PAIRS = [[2 * i, 2 * i + 1] for i in range(NZ * PLANE)]
SWAP = [(i, i ^ 1) for i in range(NZ * PLANE * NC)]


def exchange(blocks, groups):
    return lax.all_to_all(blocks, BOTH, 0, 0, axis_index_groups=groups)


def spread(block, groups):
    number = len(groups[0])
    return exchange(jnp.broadcast_to(block[None], (number,) + block.shape), groups)


def columns(a, b):
    return lax.dot_general(a, b, (((1,), (0,)), ((), ())), preferred_element_type=jnp.float32)


SLABS = 2


def block_kernel(core_ref, ga_ref, gb_ref, w_ref, pt_ref, f_ref, h_ref, x_ref, acc_ref, s_ref):
    step = pl.program_id(0)
    core = core_ref[0]
    lane16 = lax.broadcasted_iota(jnp.int32, (16, 128), 1)
    first = (lane16 < 64).astype(jnp.float32).astype(jnp.bfloat16)
    second = (lane16 >= 64).astype(jnp.float32).astype(jnp.bfloat16)
    for slab in range(SLABS):
        for place, (xl, y, xh) in enumerate(SITES):
            gx = xl * NXH + xh
            here, there = y * NX + gx, gx * NY + y
            q = here + core * (there - here)
            base = slab * 512 + place * 32
            x_ref[base : base + 32, 0:128] = ga_ref[q, slab * 32 : slab * 32 + 32, :]
            tile = gb_ref[q, slab * 16 : slab * 16 + 16, :]
            x_ref[base : base + 16, 128:256] = tile * first
            x_ref[base + 16 : base + 32, 128:256] = tile * second
    product = columns(w_ref[...], x_ref[...])

    @pl.when(step == 0)
    def _():
        acc_ref[...] = product

    @pl.when(step > 0)
    def _():
        acc_ref[...] += product

    @pl.when(step == pl.num_programs(0) - 1)
    def _():
        def rows(start, size, lanes):
            return acc_ref[start : start + size, lanes * 128 : lanes * 128 + 128]

        def both(start):
            return jnp.concatenate([rows(start, 56, 0), rows(start + 168, 56, 0)], axis=0)

        def grads(ranges):
            low = jnp.concatenate([rows(*r, 0) for r in ranges], axis=0)
            high = jnp.concatenate([rows(*r, 1) for r in ranges], axis=0)
            lane = lax.broadcasted_iota(jnp.int32, low.shape, 1)
            return jnp.where(lane < 64, pltpu.roll(low, 32, 1), high + pltpu.roll(high, 64, 1))

        gate_sum, up_sum = both(0), both(56)
        hidden_grad = grads([(112, 56), (280, 56)])
        sigmoid_gate = jax.nn.sigmoid(gate_sum)
        silu_gate = gate_sum * sigmoid_gate
        hidden = (silu_gate * up_sum).astype(jnp.bfloat16)
        gate_grad = (
            hidden_grad * up_sum * sigmoid_gate * (1.0 + gate_sum * (1.0 - sigmoid_gate))
        ).astype(jnp.bfloat16)
        up_grad = (hidden_grad * silu_gate).astype(jnp.bfloat16)
        s_ref[0:64] = columns(pt_ref[0], gate_grad)
        s_ref[64:128] = columns(pt_ref[1], up_grad)
        s_ref[128:192] = columns(pt_ref[2], hidden)
        for p in range(PLANE):
            f_ref[p, 0:8, :] = s_ref[p * 8 : p * 8 + 8, :]
            f_ref[p, 8:12, :] = s_ref[128 + p * 4 : 132 + p * 4, :]
            f_ref[p, 12:16, :] = jnp.zeros((4, 128), jnp.float32)
        h_ref[0:64] = rows(336, 64, 0)
        h_ref[64:128] = grads([(400, 64)])


def block(core, gathered, weights, projections):
    steps = NZ // SLABS
    return pl.pallas_call(
        block_kernel,
        grid=(steps,),
        in_specs=[
            pl.BlockSpec(memory_space=pltpu.SMEM),
            pl.BlockSpec((PLANE, 32 * SLABS, 128), lambda s: (0, s, 0)),
            pl.BlockSpec((PLANE, 16 * SLABS, 128), lambda s: (0, 512 // (16 * SLABS) + s, 0)),
            pl.BlockSpec((464, 512 * SLABS), lambda s: (0, s)),
            pl.BlockSpec((3, 64, 112), lambda s: (0, 0, 0)),
        ],
        out_specs=[
            pl.BlockSpec((PLANE, 16, 128), lambda s: (0, 0, 0)),
            pl.BlockSpec((128, 128), lambda s: (0, 0)),
        ],
        out_shape=[
            jax.ShapeDtypeStruct((PLANE, 16, 128), jnp.float32),
            jax.ShapeDtypeStruct((128, 128), jnp.float32),
        ],
        scratch_shapes=[
            pltpu.VMEM((512 * SLABS, 256), jnp.bfloat16),
            pltpu.VMEM((464, 256), jnp.float32),
            pltpu.VMEM((192, 128), jnp.float32),
        ],
        compiler_params=pltpu.CompilerParams(vmem_limit_bytes=24 * MIB),
        cost_estimate=pl.CostEstimate(
            flops=2 * 464 * 8192 * 256, bytes_accessed=12 * MIB, transcendentals=112 * 128
        ),
    )(core, gathered, gathered, weights, projections)


def outer_kernel(f_ref, h_ref, ids_ref, out_ref, s_ref):
    for p in range(PLANE):
        for c in range(NC):
            s_ref[p * 8 : p * 8 + 8, c * 128 : c * 128 + 128] = f_ref[p, c, 0:8, :]
            s_ref[128 + p * 4 : 132 + p * 4, c * 128 : c * 128 + 128] = f_ref[p, c, 8:12, :]
    known = jnp.concatenate([h_ref[0], h_ref[1]], axis=1)
    ids = ids_ref[...]
    sides = (
        (s_ref[0:64, :], known[0:64]),
        (s_ref[64:128, :], known[0:64]),
        (known[64:128], s_ref[128:192, :]),
    )
    for k, (left, right) in enumerate(sides):
        stacked = jnp.concatenate(
            [jnp.where(ids == d, left, 0.0) for d in range(DOCS)], axis=0
        )
        out_ref[k] = lax.dot_general(
            stacked,
            right,
            (((1,), (1,)), ((), ())),
            precision=lax.Precision.HIGHEST,
            preferred_element_type=jnp.float32,
        )


def outer(factors, known, ids):
    return pl.pallas_call(
        outer_kernel,
        out_shape=jax.ShapeDtypeStruct((3, DOCS * 64, 64), jnp.float32),
        scratch_shapes=[pltpu.VMEM((192, 256), jnp.float32)],
        compiler_params=pltpu.CompilerParams(vmem_limit_bytes=16 * MIB),
        cost_estimate=pl.CostEstimate(
            flops=2 * 3 * 512 * 256 * 64 * 6, bytes_accessed=2 * MIB, transcendentals=0
        ),
    )(factors, known, ids)


def local(
    tokens,
    out_grad,
    gate_weight,
    up_weight,
    down_weight,
    input_proj,
    output_proj,
    gate_proj,
    up_proj,
    hidden_proj,
    doc_ids,
):
    core = (lax.axis_index("mp") % NC).astype(jnp.int32).reshape(1)
    mine = tokens.T.reshape(16, NC, HALF)
    grads = out_grad.T.reshape(16, NC, HALF)
    wide = jnp.concatenate([grads[:, :, :LOW], mine], axis=2)
    rest = grads[:, :, LOW:].reshape(2, 8, NC, 64)
    rest = rest.transpose(1, 2, 0, 3).reshape(8, NC, 128)
    sent = jnp.concatenate([wide, rest], axis=0).transpose(1, 0, 2)
    sent = jnp.broadcast_to(sent[None], (NZ, NC, 24, 128)).reshape(NZ * NC, 24, 128)
    column = exchange(sent, COLUMN_GROUPS)
    wide = column[:, :16, :].reshape(512, 128)
    rest = column[:, 16:, :].reshape(NZ, NC, 8, 2, 64)
    rest = rest.transpose(0, 3, 2, 1, 4).reshape(256, 128)
    column = jnp.concatenate([wide, rest], axis=0)
    line = spread(column, FIRST_GROUPS)
    gathered = spread(line, SECOND_GROUPS).reshape(PLANE, 768, 128)

    own = jnp.concatenate([gate_weight, up_weight, down_weight], axis=0)
    weights = jnp.concatenate(
        [own, lax.ppermute(own, BOTH, SWAP), input_proj, output_proj], axis=0
    )
    turned = jnp.stack([gate_proj.T, up_proj.T, hidden_proj.T])
    turned = jnp.concatenate([turned, lax.ppermute(turned, BOTH, SWAP)], axis=2)

    factors, known = block(core, gathered, weights, turned)
    known = lax.all_gather(known, BOTH, axis=0, axis_index_groups=PAIRS)
    part = exchange(factors, PLANE_GROUPS).sum(0)
    part = spread(part, Z_GROUPS).sum(0)
    factors = spread(part, LAYER_GROUPS).reshape(PLANE, NC, 16, 128)
    ids = jnp.pad(doc_ids.reshape(NC, HALF), ((0, 0), (LOW, 0)), constant_values=-1)
    return outer(factors, known, ids.reshape(1, NC * 128)).reshape(3, DOCS, 4096)


def solution(mesh):
    return jax.shard_map(
        local,
        mesh=mesh,
        in_specs=(
            P(None, BOTH),
            P(None, BOTH),
            P(BOTH, None),
            P(BOTH, None),
            P(BOTH, None),
            P(),
            P(),
            P(BOTH, None),
            P(BOTH, None),
            P(BOTH, None),
            P(),
        ),
        out_specs=P(),
        check_vma=False,
    )
```

```python
import jax
import jax.numpy as jnp
from jax import lax
from jax.experimental import pallas as pl
from jax.experimental.pallas import tpu as pltpu
from jax.sharding import PartitionSpec as P

DOCS = 8
BOTH = ("dp", "mp")
NZ, NXL, NY, NXH, NC = 16, 2, 4, 2, 2
NX = NXL * NXH
PLANE = NX * NY
LOW = 32
HALF = 96
MIB = 1 << 20


def device(z, xl, y, xh, c):
    return (((z * NXL + xl) * NY + y) * NXH + xh) * NC + c


def along_x(z, y, c):
    return [device(z, xl, y, xh, c) for xl in range(NXL) for xh in range(NXH)]


def along_y(z, xl, xh, c):
    return [device(z, xl, y, xh, c) for y in range(NY)]


def x_groups(c):
    return [along_x(z, y, c) for z in range(NZ) for y in range(NY)]


def y_groups(c):
    return [along_y(z, xl, xh, c) for z in range(NZ) for xl in range(NXL) for xh in range(NXH)]


SITES = [(xl, y, xh) for xl in range(NXL) for y in range(NY) for xh in range(NXH)]
COLUMN_GROUPS = [[device(z, *s, c) for z in range(NZ) for c in range(NC)] for s in SITES]
Z_GROUPS = [[device(z, *s, c) for z in range(NZ)] for s in SITES for c in range(NC)]
FIRST_GROUPS = x_groups(0) + y_groups(1)
SECOND_GROUPS = y_groups(0) + x_groups(1)
PLANE_GROUPS = [[device(z, *s, c) for s in SITES] for z in range(NZ) for c in range(NC)]
LAYER_GROUPS = [[device(z, *s, c) for s in SITES for c in range(NC)] for z in range(NZ)]
PAIRS = [[2 * i, 2 * i + 1] for i in range(NZ * PLANE)]
SWAP = [(i, i ^ 1) for i in range(NZ * PLANE * NC)]


def ring(shift):
    pairs = []
    for z in range(NZ):
        for xl, y, xh in SITES:
            pairs.append((device(z, xl, y, xh, 0), device(z, xl, (y + shift) % NY, xh, 0)))
            x = (xh * NXL + xl + shift) % NX
            pairs.append((device(z, xl, y, xh, 1), device(z, x % NXL, y, x // NXL, 1)))
    return pairs


def exchange(blocks, groups):
    return lax.all_to_all(blocks, BOTH, 0, 0, axis_index_groups=groups)


def spread(block, groups):
    number = len(groups[0])
    return exchange(jnp.broadcast_to(block[None], (number,) + block.shape), groups)


def columns(a, b):
    return lax.dot_general(a, b, (((1,), (0,)), ((), ())), preferred_element_type=jnp.float32)


SHIFTS = (0, 2, 1, 3)
SLABS = 8
ROWS = 192


def block_kernel(dest_ref, *refs):
    wide_refs, rest_refs = refs[0:4], refs[4:8]
    own_ref, other_ref, in_ref, out_ref, own_low_ref, other_low_ref = refs[8:14]
    f_ref, h_ref, x_ref, acc_ref, s_ref = refs[14:]
    step = pl.program_id(0)
    lane16 = lax.broadcasted_iota(jnp.int32, (16, 128), 1)
    first = (lane16 < 64).astype(jnp.float32).astype(jnp.bfloat16)
    second = (lane16 >= 64).astype(jnp.float32).astype(jnp.bfloat16)
    for k in range(4):
        for j in range(4):
            place = dest_ref[k * 4 + j]
            for slab in range(SLABS):
                base = pl.multiple_of(slab * 512 + place, 32)
                x_ref[pl.ds(base, 32), 0:128] = wide_refs[k][j, slab * 32 : slab * 32 + 32, :]
                tile = rest_refs[k][j, slab * 16 : slab * 16 + 16, :]
                x_ref[pl.ds(base, 16), 128:256] = tile * first
                x_ref[pl.ds(pl.multiple_of(base + 16, 16), 16), 128:256] = tile * second
    left = jnp.concatenate([own_ref[...], other_ref[...], in_ref[...], out_ref[...]], axis=0)
    product = columns(left, x_ref[...])

    @pl.when(step == 0)
    def _():
        acc_ref[...] = product

    @pl.when(step > 0)
    def _():
        acc_ref[...] += product

    @pl.when(step == pl.num_programs(0) - 1)
    def _():
        def rows(start, size, lanes):
            return acc_ref[start : start + size, lanes * 128 : lanes * 128 + 128]

        def both(start):
            return jnp.concatenate([rows(start, 56, 0), rows(start + 192, 56, 0)], axis=0)

        def grads(ranges):
            low = jnp.concatenate([rows(*r, 0) for r in ranges], axis=0)
            high = jnp.concatenate([rows(*r, 1) for r in ranges], axis=0)
            lane = lax.broadcasted_iota(jnp.int32, low.shape, 1)
            return jnp.where(lane < 64, pltpu.roll(low, 32, 1), high + pltpu.roll(high, 64, 1))

        gate_sum, up_sum = both(0), both(64)
        hidden_grad = grads([(128, 56), (320, 56)])
        sigmoid_gate = jax.nn.sigmoid(gate_sum)
        silu_gate = gate_sum * sigmoid_gate
        hidden = (silu_gate * up_sum).astype(jnp.bfloat16)
        gate_grad = (
            hidden_grad * up_sum * sigmoid_gate * (1.0 + gate_sum * (1.0 - sigmoid_gate))
        ).astype(jnp.bfloat16)
        up_grad = (hidden_grad * silu_gate).astype(jnp.bfloat16)
        for n, factor in enumerate((gate_grad, up_grad, hidden)):
            start = n * 64 + 56
            projection = jnp.concatenate(
                [
                    ref[start : start + 8, m * 128 : m * 128 + 64].astype(jnp.float32)
                    for ref in (own_low_ref, other_low_ref)
                    for m in range(7)
                ],
                axis=0,
            ).astype(jnp.bfloat16)
            s_ref[n * 64 : n * 64 + 64] = lax.dot_general(
                projection,
                factor,
                (((0,), (0,)), ((), ())),
                preferred_element_type=jnp.float32,
            )
        for p in range(PLANE):
            for r in range(3):
                f_ref[p, r] = s_ref[p * 12 + r * 4 : p * 12 + r * 4 + 4, :]
        h_ref[0:64] = rows(384, 64, 0)
        h_ref[64:128] = grads([(448, 64)])


def block(dest, lines, own, other, input_proj, output_proj):
    steps = NZ // SLABS
    wide = pl.BlockSpec((4, 32 * SLABS, 128), lambda s: (0, s, 0))
    rest = pl.BlockSpec((4, 16 * SLABS, 128), lambda s: (0, 512 // (16 * SLABS) + s, 0))
    return pl.pallas_call(
        block_kernel,
        grid=(steps,),
        in_specs=[pl.BlockSpec(memory_space=pltpu.SMEM)]
        + [wide] * 4
        + [rest] * 4
        + [
            pl.BlockSpec((ROWS, 512 * SLABS), lambda s: (0, s)),
            pl.BlockSpec((ROWS, 512 * SLABS), lambda s: (0, s)),
            pl.BlockSpec((64, 512 * SLABS), lambda s: (0, s)),
            pl.BlockSpec((64, 512 * SLABS), lambda s: (0, s)),
            pl.BlockSpec((ROWS, 1024), lambda s: (0, 0)),
            pl.BlockSpec((ROWS, 1024), lambda s: (0, 0)),
        ],
        out_specs=[
            pl.BlockSpec((PLANE, 3, 4, 128), lambda s: (0, 0, 0, 0)),
            pl.BlockSpec((128, 128), lambda s: (0, 0)),
        ],
        out_shape=[
            jax.ShapeDtypeStruct((PLANE, 3, 4, 128), jnp.float32),
            jax.ShapeDtypeStruct((128, 128), jnp.float32),
        ],
        scratch_shapes=[
            pltpu.VMEM((512 * SLABS, 256), jnp.bfloat16),
            pltpu.VMEM((2 * ROWS + 128, 256), jnp.float32),
            pltpu.VMEM((192, 128), jnp.float32),
        ],
        compiler_params=pltpu.CompilerParams(vmem_limit_bytes=28 * MIB),
        cost_estimate=pl.CostEstimate(
            flops=2 * 512 * 8192 * 256, bytes_accessed=12 * MIB, transcendentals=112 * 128
        ),
    )(dest, *lines, *lines, own, other, input_proj, output_proj, own, other)


def stack_kernel(gate_ref, up_ref, down_ref, *refs):
    out_ref = refs[3]
    for n, ref in enumerate((gate_ref, up_ref, down_ref)):
        out_ref[n * 64 : n * 64 + 56, :] = ref[...]
        out_ref[n * 64 + 56 : n * 64 + 64, :] = jnp.zeros((8, out_ref.shape[1]), jnp.bfloat16)

    @pl.when(pl.program_id(0) == 0)
    def _():
        for n in range(3):
            for m in range(7):
                piece = refs[n][m * 8 : m * 8 + 8, :]
                out_ref[n * 64 + 56 : n * 64 + 64, m * 128 : m * 128 + 64] = piece


def stack(weights, projections):
    width = 2048
    weight = pl.BlockSpec((56, width), lambda s: (0, s))
    projection = pl.BlockSpec((56, 64), lambda s: (0, 0))
    return pl.pallas_call(
        stack_kernel,
        grid=(8192 // width,),
        in_specs=[weight] * 3 + [projection] * 3,
        out_specs=pl.BlockSpec((ROWS, width), lambda s: (0, s)),
        out_shape=jax.ShapeDtypeStruct((ROWS, 8192), jnp.bfloat16),
        cost_estimate=pl.CostEstimate(flops=0, bytes_accessed=6 * MIB, transcendentals=0),
    )(*weights, *projections)


def pack_kernel(t_ref, g_ref, out_ref):
    t, g = t_ref[...].astype(jnp.float32), g_ref[...].astype(jnp.float32)
    for c in range(NC):
        start = c * HALF
        mine = jnp.concatenate([g[:, start : start + LOW], t[:, start : start + HALF]], axis=1)
        rest = g[:, start + LOW : start + HALF]
        rest = jnp.concatenate([rest[0:8], rest[8:16]], axis=1)
        packed = jnp.concatenate([mine, rest], axis=0).astype(jnp.bfloat16)
        for z in range(NZ):
            out_ref[z * NC + c] = packed


def pack(tokens, out_grad):
    return pl.pallas_call(
        pack_kernel,
        out_shape=jax.ShapeDtypeStruct((NZ * NC, 24, 128), jnp.bfloat16),
        cost_estimate=pl.CostEstimate(flops=0, bytes_accessed=1 << 18, transcendentals=0),
    )(tokens, out_grad)


def unpack_kernel(column_ref, out_ref):
    left = lax.broadcasted_iota(jnp.int32, (8, 128), 1) < 64
    for z in range(NZ):
        halves = []
        for c in range(NC):
            block = column_ref[z * NC + c].astype(jnp.float32)
            halves.append(block[16:24])
            for n in range(4):
                row = (z * NC + c) * 16
                out_ref[n, row : row + 16, :] = block[0:16].astype(jnp.bfloat16)
        top = jnp.where(left, halves[0], pltpu.roll(halves[1], 64, 1))
        low = jnp.where(left, pltpu.roll(halves[0], 64, 1), halves[1])
        rest = jnp.concatenate([top, low], axis=0).astype(jnp.bfloat16)
        for n in range(4):
            out_ref[n, 512 + z * 16 : 528 + z * 16, :] = rest


def unpack(column):
    return pl.pallas_call(
        unpack_kernel,
        out_shape=jax.ShapeDtypeStruct((4, 768, 128), jnp.bfloat16),
        cost_estimate=pl.CostEstimate(flops=0, bytes_accessed=MIB, transcendentals=0),
    )(column)


def outer_kernel(f_ref, h_ref, ids_ref, out_ref, s_ref):
    for p in range(PLANE):
        for c in range(NC):
            for r in range(3):
                row = p * 12 + r * 4
                s_ref[row : row + 4, c * 128 : c * 128 + 128] = f_ref[p, c, r]
    known = jnp.concatenate([h_ref[0], h_ref[1]], axis=1)
    doc = lax.broadcasted_iota(jnp.int32, (DOCS, NC * 128), 0)
    inside = (ids_ref[...] == doc)[None]
    sides = (
        (s_ref[0:64, :], known[0:64]),
        (s_ref[64:128, :], known[0:64]),
        (known[64:128], s_ref[128:192, :]),
    )
    for k, (left, right) in enumerate(sides):
        stacked = jnp.where(inside, left[:, None, :], 0.0).reshape(64 * DOCS, NC * 128)
        blocks = lax.dot_general(
            stacked,
            right,
            (((1,), (1,)), ((), ())),
            precision=lax.Precision.HIGHEST,
            preferred_element_type=jnp.float32,
        )
        for i in range(0, 64, 2):
            pair = [blocks[(i + n) * DOCS : (i + n + 1) * DOCS] for n in range(2)]
            out_ref[k, :, i * 64 : i * 64 + 128] = jnp.concatenate(pair, axis=1)


def outer(factors, known, ids):
    return pl.pallas_call(
        outer_kernel,
        out_shape=jax.ShapeDtypeStruct((3, DOCS, 4096), jnp.float32),
        scratch_shapes=[pltpu.VMEM((192, 256), jnp.float32)],
        compiler_params=pltpu.CompilerParams(vmem_limit_bytes=16 * MIB),
        cost_estimate=pl.CostEstimate(
            flops=2 * 3 * 512 * 256 * 64 * 6, bytes_accessed=2 * MIB, transcendentals=0
        ),
    )(factors, known, ids)


def local(
    tokens,
    out_grad,
    gate_weight,
    up_weight,
    down_weight,
    input_proj,
    output_proj,
    gate_proj,
    up_proj,
    hidden_proj,
    doc_ids,
):
    me = lax.axis_index("dp") * 16 + lax.axis_index("mp")
    core, x, y = me % NC, me // 2 % NXH * NXL + me // 16 % NXL, me // 4 % NY
    column = exchange(pack(tokens.T, out_grad.T), COLUMN_GROUPS)
    line = exchange(unpack(column), FIRST_GROUPS)
    lines = [line] + [lax.ppermute(line, BOTH, ring(shift)) for shift in SHIFTS[1:]]
    dest = []
    for shift in SHIFTS:
        from_y, from_x = (y - shift) % NY, (x - shift) % NX
        for j in range(4):
            even = j // NXH * 8 + from_y * 2 + j % NXH
            odd = from_x % NXL * 8 + j * 2 + from_x // NXL
            dest.append(jnp.where(core == 0, even, odd) * 32)
    dest = jnp.stack(dest).astype(jnp.int32)

    own = stack((gate_weight, up_weight, down_weight), (gate_proj, up_proj, hidden_proj))
    other = lax.ppermute(own, BOTH, SWAP)

    factors, known = block(dest, lines, own, other, input_proj, output_proj)
    known = lax.all_gather(known, BOTH, axis=0, axis_index_groups=PAIRS)
    part = exchange(factors, PLANE_GROUPS).sum(0)
    part = spread(part, Z_GROUPS).sum(0)
    factors = spread(part, LAYER_GROUPS).reshape(PLANE, NC, 3, 4, 128)
    ids = jnp.pad(doc_ids.reshape(NC, HALF), ((0, 0), (LOW, 0)), constant_values=-1)
    return outer(factors, known, ids.reshape(1, NC * 128))


def solution(mesh):
    return jax.shard_map(
        local,
        mesh=mesh,
        in_specs=(
            P(None, BOTH),
            P(None, BOTH),
            P(BOTH, None),
            P(BOTH, None),
            P(BOTH, None),
            P(),
            P(),
            P(BOTH, None),
            P(BOTH, None),
            P(BOTH, None),
            P(),
        ),
        out_specs=P(),
        check_vma=False,
    )
```

```python
import jax
import jax.numpy as jnp
from jax import lax
from jax.experimental import pallas as pl
from jax.experimental.pallas import tpu as pltpu
from jax.sharding import PartitionSpec as P

DOCS = 8
BOTH = ("dp", "mp")
NZ, NXL, NY, NXH, NC = 16, 2, 4, 2, 2
NX = NXL * NXH
PLANE = NX * NY
LOW = 32
HALF = 96
MIB = 1 << 20


def device(z, xl, y, xh, c):
    return (((z * NXL + xl) * NY + y) * NXH + xh) * NC + c


def along_x(z, y, c):
    return [device(z, xl, y, xh, c) for xl in range(NXL) for xh in range(NXH)]


def along_y(z, xl, xh, c):
    return [device(z, xl, y, xh, c) for y in range(NY)]


def x_groups(c):
    return [along_x(z, y, c) for z in range(NZ) for y in range(NY)]


def y_groups(c):
    return [along_y(z, xl, xh, c) for z in range(NZ) for xl in range(NXL) for xh in range(NXH)]


SITES = [(xl, y, xh) for xl in range(NXL) for y in range(NY) for xh in range(NXH)]
COLUMN_GROUPS = [[device(z, *s, c) for z in range(NZ) for c in range(NC)] for s in SITES]
Z_GROUPS = [[device(z, *s, c) for z in range(NZ)] for s in SITES for c in range(NC)]
FIRST_GROUPS = x_groups(0) + y_groups(1)
SECOND_GROUPS = y_groups(0) + x_groups(1)
PLANE_GROUPS = [[device(z, *s, c) for s in SITES] for z in range(NZ) for c in range(NC)]
LAYER_GROUPS = [[device(z, *s, c) for s in SITES for c in range(NC)] for z in range(NZ)]
PAIRS = [[2 * i, 2 * i + 1] for i in range(NZ * PLANE)]
SWAP = [(i, i ^ 1) for i in range(NZ * PLANE * NC)]


def ring(shift):
    pairs = []
    for z in range(NZ):
        for xl, y, xh in SITES:
            pairs.append((device(z, xl, y, xh, 0), device(z, xl, (y + shift) % NY, xh, 0)))
            x = (xh * NXL + xl + shift) % NX
            pairs.append((device(z, xl, y, xh, 1), device(z, x % NXL, y, x // NXL, 1)))
    return pairs


def exchange(blocks, groups):
    return lax.all_to_all(blocks, BOTH, 0, 0, axis_index_groups=groups)


def spread(block, groups):
    number = len(groups[0])
    return exchange(jnp.broadcast_to(block[None], (number,) + block.shape), groups)


def columns(a, b):
    return lax.dot_general(a, b, (((1,), (0,)), ((), ())), preferred_element_type=jnp.float32)


SHIFTS = (0, 2, 1, 3)
ROWS = 192
ALL_ROWS = 2 * ROWS + 2 * 64
GROUPS = 4
SLABS = NZ // GROUPS


def block_kernel(dest_ref, *refs):
    lines, w_ref, f_ref, h_ref, x_ref, acc_ref, s_ref = refs[0:4], *refs[4:]
    lane16 = lax.broadcasted_iota(jnp.int32, (16, 128), 1)
    first = (lane16 < 64).astype(jnp.float32).astype(jnp.bfloat16)
    second = (lane16 >= 64).astype(jnp.float32).astype(jnp.bfloat16)
    for group in range(GROUPS):
        for k in range(4):
            for j in range(4):
                place = dest_ref[k * 4 + j]
                for slab in range(group * SLABS, group * SLABS + SLABS):
                    base = pl.multiple_of(slab * 512 + place, 32)
                    x_ref[pl.ds(base, 32), 0:128] = lines[k][j, slab * 32 : slab * 32 + 32, :]
                    tile = lines[k][j, 512 + slab * 16 : 528 + slab * 16, :]
                    x_ref[pl.ds(base, 16), 128:256] = tile * first
                    x_ref[pl.ds(pl.multiple_of(base + 16, 16), 16), 128:256] = tile * second
        span = slice(group * SLABS * 512, (group + 1) * SLABS * 512)
        product = columns(w_ref[:, span], x_ref[span, :])
        if group == 0:
            acc_ref[...] = product
        else:
            acc_ref[...] += product

    def rows(start, size, lanes):
        return acc_ref[start : start + size, lanes * 128 : lanes * 128 + 128]

    def both(start):
        return jnp.concatenate([rows(start, 56, 0), rows(start + 192, 56, 0)], axis=0)

    def grads(ranges):
        low = jnp.concatenate([rows(*r, 0) for r in ranges], axis=0)
        high = jnp.concatenate([rows(*r, 1) for r in ranges], axis=0)
        lane = lax.broadcasted_iota(jnp.int32, low.shape, 1)
        return jnp.where(lane < 64, pltpu.roll(low, 32, 1), high + pltpu.roll(high, 64, 1))

    gate_sum, up_sum = both(0), both(64)
    hidden_grad = grads([(128, 56), (320, 56)])
    sigmoid_gate = jax.nn.sigmoid(gate_sum)
    silu_gate = gate_sum * sigmoid_gate
    hidden = (silu_gate * up_sum).astype(jnp.bfloat16)
    gate_grad = (
        hidden_grad * up_sum * sigmoid_gate * (1.0 + gate_sum * (1.0 - sigmoid_gate))
    ).astype(jnp.bfloat16)
    up_grad = (hidden_grad * silu_gate).astype(jnp.bfloat16)
    for n, factor in enumerate((gate_grad, up_grad, hidden)):
        start = n * 64 + 56
        projection = jnp.concatenate(
            [
                w_ref[base + start : base + start + 8, m * 128 : m * 128 + 64].astype(jnp.float32)
                for base in (0, ROWS)
                for m in range(7)
            ],
            axis=0,
        ).astype(jnp.bfloat16)
        s_ref[n * 64 : n * 64 + 64] = lax.dot_general(
            projection,
            factor,
            (((0,), (0,)), ((), ())),
            preferred_element_type=jnp.float32,
        )
    for p in range(PLANE):
        for r in range(3):
            f_ref[p, r] = s_ref[p * 12 + r * 4 : p * 12 + r * 4 + 4, :]
    h_ref[0:64] = rows(384, 64, 0)
    h_ref[64:128] = grads([(448, 64)])


def block(dest, lines, weights):
    inside = pl.BlockSpec(memory_space=pltpu.VMEM)
    return pl.pallas_call(
        block_kernel,
        in_specs=[pl.BlockSpec(memory_space=pltpu.SMEM)] + [inside] * 5,
        out_specs=[inside] * 2,
        out_shape=[
            jax.ShapeDtypeStruct((PLANE, 3, 4, 128), jnp.float32),
            jax.ShapeDtypeStruct((128, 128), jnp.float32),
        ],
        scratch_shapes=[
            pltpu.VMEM((8192, 256), jnp.bfloat16),
            pltpu.VMEM((ALL_ROWS, 256), jnp.float32),
            pltpu.VMEM((192, 128), jnp.float32),
        ],
        compiler_params=pltpu.CompilerParams(vmem_limit_bytes=24 * MIB),
        cost_estimate=pl.CostEstimate(
            flops=2 * ALL_ROWS * 8192 * 256, bytes_accessed=12 * MIB, transcendentals=112 * 128
        ),
    )(dest, *lines, weights)


def load_kernel(*refs):
    parts, w_ref, sems = refs[0:8], *refs[9:]
    copies = []
    for n, part in enumerate(parts):
        copies.append(pltpu.make_async_copy(part, w_ref.at[pl.ds(n * 64, 64)], sems.at[n]))
    for copy in copies:
        copy.start()
    for copy in copies:
        copy.wait()


def load(parts, after):
    return pl.pallas_call(
        load_kernel,
        in_specs=[pl.BlockSpec(memory_space=pl.ANY)] * 9,
        out_specs=pl.BlockSpec(memory_space=pltpu.VMEM),
        out_shape=pltpu.VMEM((ALL_ROWS, 8192), jnp.bfloat16),
        scratch_shapes=[pltpu.SemaphoreType.DMA((8,))],
        compiler_params=pltpu.CompilerParams(vmem_limit_bytes=16 * MIB),
        cost_estimate=pl.CostEstimate(flops=0, bytes_accessed=16 * MIB, transcendentals=0),
    )(*parts, after)


def stack_kernel(*refs):
    weights, projections, outs = refs[0:3], refs[3:6], refs[6:9]
    for weight, out in zip(weights, outs):
        out[0:56, :] = weight[...]
        out[56:64, :] = jnp.zeros((8, out.shape[1]), jnp.bfloat16)

    @pl.when(pl.program_id(0) == 0)
    def _():
        for projection, out in zip(projections, outs):
            for m in range(7):
                out[56:64, m * 128 : m * 128 + 64] = projection[m * 8 : m * 8 + 8, :]


def stack(weights, projections):
    width = 2048
    weight = pl.BlockSpec((56, width), lambda s: (0, s))
    projection = pl.BlockSpec((56, 64), lambda s: (0, 0))
    return pl.pallas_call(
        stack_kernel,
        grid=(8192 // width,),
        in_specs=[weight] * 3 + [projection] * 3,
        out_specs=[pl.BlockSpec((64, width), lambda s: (0, s))] * 3,
        out_shape=[jax.ShapeDtypeStruct((64, 8192), jnp.bfloat16)] * 3,
        cost_estimate=pl.CostEstimate(flops=0, bytes_accessed=6 * MIB, transcendentals=0),
    )(*weights, *projections)


def pack_kernel(t_ref, g_ref, out_ref):
    t, g = t_ref[...].astype(jnp.float32), g_ref[...].astype(jnp.float32)
    for c in range(NC):
        start = c * HALF
        mine = jnp.concatenate([g[:, start : start + LOW], t[:, start : start + HALF]], axis=1)
        rest = g[:, start + LOW : start + HALF]
        rest = jnp.concatenate([rest[0:8], rest[8:16]], axis=1)
        packed = jnp.concatenate([mine, rest], axis=0).astype(jnp.bfloat16)
        for z in range(NZ):
            out_ref[z * NC + c] = packed


def pack(tokens, out_grad):
    return pl.pallas_call(
        pack_kernel,
        out_shape=jax.ShapeDtypeStruct((NZ * NC, 24, 128), jnp.bfloat16),
        cost_estimate=pl.CostEstimate(flops=0, bytes_accessed=1 << 18, transcendentals=0),
    )(tokens, out_grad)


def outer_kernel(f_ref, h_ref, ids_ref, out_ref, s_ref):
    for p in range(PLANE):
        for c in range(NC):
            for r in range(3):
                row = p * 12 + r * 4
                s_ref[row : row + 4, c * 128 : c * 128 + 128] = f_ref[p, c, r]
    known = jnp.concatenate([h_ref[0], h_ref[1]], axis=1)
    doc = lax.broadcasted_iota(jnp.int32, (DOCS, NC * 128), 0)
    inside = (ids_ref[...] == doc)[None]
    sides = (
        (s_ref[0:64, :], known[0:64]),
        (s_ref[64:128, :], known[0:64]),
        (known[64:128], s_ref[128:192, :]),
    )
    for k, (left, right) in enumerate(sides):
        stacked = jnp.where(inside, left[:, None, :], 0.0).reshape(64 * DOCS, NC * 128)
        blocks = lax.dot_general(
            stacked,
            right,
            (((1,), (1,)), ((), ())),
            precision=lax.Precision.HIGHEST,
            preferred_element_type=jnp.float32,
        )
        for i in range(0, 64, 2):
            pair = [blocks[(i + n) * DOCS : (i + n + 1) * DOCS] for n in range(2)]
            out_ref[k, :, i * 64 : i * 64 + 128] = jnp.concatenate(pair, axis=1)


def outer(factors, known, ids):
    return pl.pallas_call(
        outer_kernel,
        out_shape=jax.ShapeDtypeStruct((3, DOCS, 4096), jnp.float32),
        scratch_shapes=[pltpu.VMEM((192, 256), jnp.float32)],
        compiler_params=pltpu.CompilerParams(vmem_limit_bytes=16 * MIB),
        cost_estimate=pl.CostEstimate(
            flops=2 * 3 * 512 * 256 * 64 * 6, bytes_accessed=2 * MIB, transcendentals=0
        ),
    )(factors, known, ids)


def local(
    tokens,
    out_grad,
    gate_weight,
    up_weight,
    down_weight,
    input_proj,
    output_proj,
    gate_proj,
    up_proj,
    hidden_proj,
    doc_ids,
):
    me = lax.axis_index("dp") * 16 + lax.axis_index("mp")
    core, x, y = me % NC, me // 2 % NXH * NXL + me // 16 % NXL, me // 4 % NY
    column = exchange(pack(tokens.T, out_grad.T), COLUMN_GROUPS)
    wide = column[:, :16, :].reshape(512, 128)
    rest = column[:, 16:, :].reshape(NZ, NC, 8, 2, 64)
    rest = rest.transpose(0, 3, 2, 1, 4).reshape(256, 128)
    column = jnp.concatenate([wide, rest], axis=0)
    own = stack((gate_weight, up_weight, down_weight), (gate_proj, up_proj, hidden_proj))
    other = [lax.ppermute(part, BOTH, SWAP) for part in own]
    line = spread(column, FIRST_GROUPS)
    lines = [line] + [lax.ppermute(line, BOTH, ring(shift)) for shift in SHIFTS[1:]]
    dest = []
    for shift in SHIFTS:
        from_y, from_x = (y - shift) % NY, (x - shift) % NX
        for j in range(4):
            even = j // NXH * 8 + from_y * 2 + j % NXH
            odd = from_x % NXL * 8 + j * 2 + from_x // NXL
            dest.append(jnp.where(core == 0, even, odd) * 32)
    dest = jnp.stack(dest).astype(jnp.int32)

    weights = load((*own, *other, input_proj, output_proj), line)
    factors, known = block(dest, lines, weights)
    known = lax.all_gather(known, BOTH, axis=0, axis_index_groups=PAIRS)
    part = exchange(factors, PLANE_GROUPS).sum(0)
    part = spread(part, Z_GROUPS).sum(0)
    factors = spread(part, LAYER_GROUPS).reshape(PLANE, NC, 3, 4, 128)
    ids = jnp.pad(doc_ids.reshape(NC, HALF), ((0, 0), (LOW, 0)), constant_values=-1)
    return outer(factors, known, ids.reshape(1, NC * 128))


def solution(mesh):
    return jax.shard_map(
        local,
        mesh=mesh,
        in_specs=(
            P(None, BOTH),
            P(None, BOTH),
            P(BOTH, None),
            P(BOTH, None),
            P(BOTH, None),
            P(),
            P(),
            P(BOTH, None),
            P(BOTH, None),
            P(BOTH, None),
            P(),
        ),
        out_specs=P(),
        check_vma=False,
    )
```

```python
import jax
import jax.numpy as jnp
from jax import lax
from jax.experimental import pallas as pl
from jax.experimental.pallas import tpu as pltpu
from jax.sharding import PartitionSpec as P

DOCS = 8
BOTH = ("dp", "mp")
NZ, NXL, NY, NXH, NC = 16, 2, 4, 2, 2
NX = NXL * NXH
PLANE = NX * NY
LOW = 32
HALF = 96
MIB = 1 << 20


def device(z, xl, y, xh, c):
    return (((z * NXL + xl) * NY + y) * NXH + xh) * NC + c


def along_x(z, y, c):
    return [device(z, xl, y, xh, c) for xl in range(NXL) for xh in range(NXH)]


def along_y(z, xl, xh, c):
    return [device(z, xl, y, xh, c) for y in range(NY)]


def x_groups(c):
    return [along_x(z, y, c) for z in range(NZ) for y in range(NY)]


def y_groups(c):
    return [along_y(z, xl, xh, c) for z in range(NZ) for xl in range(NXL) for xh in range(NXH)]


SITES = [(xl, y, xh) for xl in range(NXL) for y in range(NY) for xh in range(NXH)]
ORDER = [(z + NZ // 2) % NZ for z in range(NZ)]
COLUMN_GROUPS = [[device(z, *s, c) for z in ORDER for c in range(NC)] for s in SITES]
Z_GROUPS = [[device(z, *s, c) for z in ORDER] for s in SITES for c in range(NC)]
FIRST_GROUPS = x_groups(0) + y_groups(1)
SECOND_GROUPS = y_groups(0) + x_groups(1)
PLANE_GROUPS = [[device(z, *s, c) for s in SITES] for z in range(NZ) for c in range(NC)]
LAYER_GROUPS = [[device(z, *s, c) for s in SITES for c in range(NC)] for z in range(NZ)]
PAIRS = [[2 * i, 2 * i + 1] for i in range(NZ * PLANE)]
SWAP = [(i, i ^ 1) for i in range(NZ * PLANE * NC)]


def ring(shift):
    pairs = []
    for z in range(NZ):
        for xl, y, xh in SITES:
            pairs.append((device(z, xl, y, xh, 0), device(z, xl, (y + shift) % NY, xh, 0)))
            x = (xh * NXL + xl + shift) % NX
            pairs.append((device(z, xl, y, xh, 1), device(z, x % NXL, y, x // NXL, 1)))
    return pairs


def exchange(blocks, groups):
    return lax.all_to_all(blocks, BOTH, 0, 0, axis_index_groups=groups)


def spread(block, groups):
    number = len(groups[0])
    return exchange(jnp.broadcast_to(block[None], (number,) + block.shape), groups)


def columns(a, b):
    return lax.dot_general(a, b, (((1,), (0,)), ((), ())), preferred_element_type=jnp.float32)


SHIFTS = (0, 2, 1, 3)
ROWS = 192
ALL_ROWS = 2 * ROWS + 2 * 64
GROUPS = 4
SLABS = NZ // GROUPS


def block_kernel(dest_ref, *refs):
    lines = refs[0:4]
    w_ref, f_ref, h_ref, x_ref, acc_ref, s_ref = refs[4:]
    lane16 = lax.broadcasted_iota(jnp.int32, (16, 128), 1)
    first = (lane16 < 64).astype(jnp.float32).astype(jnp.bfloat16)
    second = (lane16 >= 64).astype(jnp.float32).astype(jnp.bfloat16)
    for group in range(GROUPS):
        for k in range(4):
            for j in range(4):
                place = dest_ref[k * 4 + j]
                for z in range(group * SLABS, group * SLABS + SLABS):
                    slab = ORDER.index(z)
                    base = pl.multiple_of(z * 512 + place, 32)
                    x_ref[pl.ds(base, 32), 0:128] = lines[k][j, slab * 32 : slab * 32 + 32, :]
                    tile = lines[k][j, 512 + slab * 16 : 528 + slab * 16, :]
                    x_ref[pl.ds(base, 16), 128:256] = tile * first
                    x_ref[pl.ds(pl.multiple_of(base + 16, 16), 16), 128:256] = tile * second
        span = slice(group * SLABS * 512, (group + 1) * SLABS * 512)
        product = columns(w_ref[:, span], x_ref[span, :])
        if group == 0:
            acc_ref[...] = product
        else:
            acc_ref[...] += product

    def rows(start, size, lanes):
        return acc_ref[start : start + size, lanes * 128 : lanes * 128 + 128]

    def both(start):
        return jnp.concatenate([rows(start, 56, 0), rows(start + 192, 56, 0)], axis=0)

    def grads(ranges):
        low = jnp.concatenate([rows(*r, 0) for r in ranges], axis=0)
        high = jnp.concatenate([rows(*r, 1) for r in ranges], axis=0)
        lane = lax.broadcasted_iota(jnp.int32, low.shape, 1)
        return jnp.where(lane < 64, pltpu.roll(low, 32, 1), high + pltpu.roll(high, 64, 1))

    gate_sum, up_sum = both(0), both(64)
    hidden_grad = grads([(128, 56), (320, 56)])
    sigmoid_gate = jax.nn.sigmoid(gate_sum)
    silu_gate = gate_sum * sigmoid_gate
    hidden = (silu_gate * up_sum).astype(jnp.bfloat16)
    gate_grad = (
        hidden_grad * up_sum * sigmoid_gate * (1.0 + gate_sum * (1.0 - sigmoid_gate))
    ).astype(jnp.bfloat16)
    up_grad = (hidden_grad * silu_gate).astype(jnp.bfloat16)
    for n, factor in enumerate((gate_grad, up_grad, hidden)):
        start = n * 64 + 56
        projection = jnp.concatenate(
            [
                w_ref[base + start : base + start + 8, m * 128 : m * 128 + 64].astype(jnp.float32)
                for base in (0, ROWS)
                for m in range(7)
            ],
            axis=0,
        ).astype(jnp.bfloat16)
        s_ref[n * 64 : n * 64 + 64] = lax.dot_general(
            projection,
            factor,
            (((0,), (0,)), ((), ())),
            preferred_element_type=jnp.float32,
        )
    for p in range(PLANE):
        for r in range(3):
            f_ref[p, r] = s_ref[p * 12 + r * 4 : p * 12 + r * 4 + 4, :]
    h_ref[0:64] = rows(384, 64, 0)
    h_ref[64:128] = grads([(448, 64)])


def block(dest, lines, weights):
    inside = pl.BlockSpec(memory_space=pltpu.VMEM)
    return pl.pallas_call(
        block_kernel,
        in_specs=[pl.BlockSpec(memory_space=pltpu.SMEM)] + [inside] * 5,
        out_specs=[inside] * 2,
        out_shape=[
            jax.ShapeDtypeStruct((PLANE, 3, 4, 128), jnp.float32),
            jax.ShapeDtypeStruct((128, 128), jnp.float32),
        ],
        scratch_shapes=[
            pltpu.VMEM((8192, 256), jnp.bfloat16),
            pltpu.VMEM((ALL_ROWS, 256), jnp.float32),
            pltpu.VMEM((192, 128), jnp.float32),
        ],
        compiler_params=pltpu.CompilerParams(vmem_limit_bytes=24 * MIB),
        cost_estimate=pl.CostEstimate(
            flops=2 * ALL_ROWS * 8192 * 256, bytes_accessed=12 * MIB, transcendentals=112 * 128
        ),
    )(dest, *lines, weights)


def load_kernel(*refs):
    parts, w_ref, sems = refs[0:8], *refs[9:]
    copies = []
    for n, part in enumerate(parts):
        copies.append(pltpu.make_async_copy(part, w_ref.at[pl.ds(n * 64, 64)], sems.at[n]))
    for copy in copies:
        copy.start()
    for copy in copies:
        copy.wait()


def load(parts, after):
    return pl.pallas_call(
        load_kernel,
        in_specs=[pl.BlockSpec(memory_space=pl.ANY)] * 9,
        out_specs=pl.BlockSpec(memory_space=pltpu.VMEM),
        out_shape=pltpu.VMEM((ALL_ROWS, 8192), jnp.bfloat16),
        scratch_shapes=[pltpu.SemaphoreType.DMA((8,))],
        compiler_params=pltpu.CompilerParams(vmem_limit_bytes=16 * MIB),
        cost_estimate=pl.CostEstimate(flops=0, bytes_accessed=16 * MIB, transcendentals=0),
    )(*[pltpu.with_memory_space_constraint(part, pltpu.HBM) for part in parts], after)


def stack_kernel(*refs):
    weights, projections, outs = refs[0:3], refs[3:6], refs[6:9]
    for weight, out in zip(weights, outs):
        out[0:56, :] = weight[...]
        out[56:64, :] = jnp.zeros((8, out.shape[1]), jnp.bfloat16)

    @pl.when(pl.program_id(0) == 0)
    def _():
        for projection, out in zip(projections, outs):
            for m in range(7):
                out[56:64, m * 128 : m * 128 + 64] = projection[m * 8 : m * 8 + 8, :]


def stack(weights, projections):
    width = 2048
    weight = pl.BlockSpec((56, width), lambda s: (0, s))
    projection = pl.BlockSpec((56, 64), lambda s: (0, 0))
    return pl.pallas_call(
        stack_kernel,
        grid=(8192 // width,),
        in_specs=[weight] * 3 + [projection] * 3,
        out_specs=[pl.BlockSpec((64, width), lambda s: (0, s))] * 3,
        out_shape=[jax.ShapeDtypeStruct((64, 8192), jnp.bfloat16)] * 3,
        cost_estimate=pl.CostEstimate(flops=0, bytes_accessed=6 * MIB, transcendentals=0),
    )(*weights, *projections)


def pack_kernel(t_ref, g_ref, out_ref):
    t, g = t_ref[...].astype(jnp.float32), g_ref[...].astype(jnp.float32)
    for c in range(NC):
        start = c * HALF
        mine = jnp.concatenate([g[:, start : start + LOW], t[:, start : start + HALF]], axis=1)
        rest = g[:, start + LOW : start + HALF]
        rest = jnp.concatenate([rest[0:8], rest[8:16]], axis=1)
        packed = jnp.concatenate([mine, rest], axis=0).astype(jnp.bfloat16)
        for z in range(NZ):
            out_ref[z * NC + c] = packed


def pack(tokens, out_grad):
    return pl.pallas_call(
        pack_kernel,
        out_shape=jax.ShapeDtypeStruct((NZ * NC, 24, 128), jnp.bfloat16),
        cost_estimate=pl.CostEstimate(flops=0, bytes_accessed=1 << 18, transcendentals=0),
    )(tokens, out_grad)


def outer_kernel(f_ref, h_ref, ids_ref, out_ref, s_ref):
    for p in range(PLANE):
        for c in range(NC):
            for r in range(3):
                row = p * 12 + r * 4
                s_ref[row : row + 4, c * 128 : c * 128 + 128] = f_ref[p, c, r]
    known = jnp.concatenate([h_ref[0], h_ref[1]], axis=1)
    doc = lax.broadcasted_iota(jnp.int32, (DOCS, NC * 128), 0)
    inside = (ids_ref[...] == doc)[None]
    sides = (
        (s_ref[0:64, :], known[0:64]),
        (s_ref[64:128, :], known[0:64]),
        (known[64:128], s_ref[128:192, :]),
    )
    def parts(side):
        high = side.astype(jnp.bfloat16).astype(jnp.float32)
        return high, side - high

    for k, (left, right) in enumerate(sides):
        left_high, left_low = [
            jnp.where(inside, part[:, None, :], 0.0)
            .reshape(64 * DOCS, NC * 128)
            .astype(jnp.bfloat16)
            for part in parts(left)
        ]
        right_high, right_low = [part.astype(jnp.bfloat16) for part in parts(right)]
        blocks = lax.dot_general(
            jnp.concatenate([left_high, left_high, left_low], axis=1),
            jnp.concatenate([right_high, right_low, right_high], axis=1),
            (((1,), (1,)), ((), ())),
            preferred_element_type=jnp.float32,
        )
        for i in range(0, 64, 2):
            pair = [blocks[(i + n) * DOCS : (i + n + 1) * DOCS] for n in range(2)]
            out_ref[k, :, i * 64 : i * 64 + 128] = jnp.concatenate(pair, axis=1)


def outer(factors, known, ids):
    return pl.pallas_call(
        outer_kernel,
        out_shape=jax.ShapeDtypeStruct((3, DOCS, 4096), jnp.float32),
        scratch_shapes=[pltpu.VMEM((192, 256), jnp.float32)],
        compiler_params=pltpu.CompilerParams(vmem_limit_bytes=16 * MIB),
        cost_estimate=pl.CostEstimate(
            flops=2 * 3 * 512 * 256 * 64 * 3, bytes_accessed=2 * MIB, transcendentals=0
        ),
    )(factors, known, ids)


def local(
    tokens,
    out_grad,
    gate_weight,
    up_weight,
    down_weight,
    input_proj,
    output_proj,
    gate_proj,
    up_proj,
    hidden_proj,
    doc_ids,
):
    me = lax.axis_index("dp") * 16 + lax.axis_index("mp")
    core, x, y = me % NC, me // 2 % NXH * NXL + me // 16 % NXL, me // 4 % NY
    column = exchange(pack(tokens.T, out_grad.T), COLUMN_GROUPS)
    wide = column[:, :16, :].reshape(512, 128)
    rest = column[:, 16:, :].reshape(NZ, NC, 8, 2, 64)
    rest = rest.transpose(0, 3, 2, 1, 4).reshape(256, 128)
    column = jnp.concatenate([wide, rest], axis=0)
    own = stack((gate_weight, up_weight, down_weight), (gate_proj, up_proj, hidden_proj))
    other = [lax.ppermute(part, BOTH, SWAP) for part in own]
    line = spread(column, FIRST_GROUPS)
    line, *other = lax.optimization_barrier((line, *other))
    lines = [line] + [lax.ppermute(line, BOTH, ring(shift)) for shift in SHIFTS[1:]]
    dest = []
    for shift in SHIFTS:
        from_y, from_x = (y - shift) % NY, (x - shift) % NX
        for j in range(4):
            even = j // NXH * 8 + from_y * 2 + j % NXH
            odd = from_x % NXL * 8 + j * 2 + from_x // NXL
            dest.append(jnp.where(core == 0, even, odd) * 32)
    dest = jnp.stack(dest).astype(jnp.int32)

    weights = load((*own, *other, input_proj, output_proj), line)
    factors, known = block(dest, lines, weights)
    known = lax.all_gather(known, BOTH, axis=0, axis_index_groups=PAIRS)
    part = exchange(factors, PLANE_GROUPS).sum(0)
    part = spread(part, Z_GROUPS).sum(0)
    factors = spread(part, LAYER_GROUPS).reshape(PLANE, NC, 3, 4, 128)
    ids = jnp.pad(doc_ids.reshape(NC, HALF), ((0, 0), (LOW, 0)), constant_values=-1)
    return outer(factors, known, ids.reshape(1, NC * 128))


def solution(mesh):
    return jax.shard_map(
        local,
        mesh=mesh,
        in_specs=(
            P(None, BOTH),
            P(None, BOTH),
            P(BOTH, None),
            P(BOTH, None),
            P(BOTH, None),
            P(),
            P(),
            P(BOTH, None),
            P(BOTH, None),
            P(BOTH, None),
            P(),
        ),
        out_specs=P(),
        check_vma=False,
    )
```

```python
import jax
import jax.numpy as jnp
from jax import lax
from jax.experimental import pallas as pl
from jax.experimental.pallas import tpu as pltpu
from jax.sharding import PartitionSpec as P

DOCS = 8
BOTH = ("dp", "mp")
NZ, NXL, NY, NXH, NC = 16, 2, 4, 2, 2
NX = NXL * NXH
PLANE = NX * NY
LOW = 32
HALF = 96
MIB = 1 << 20


def device(z, xl, y, xh, c):
    return (((z * NXL + xl) * NY + y) * NXH + xh) * NC + c


def along_x(z, y, c):
    return [device(z, xl, y, xh, c) for xl in range(NXL) for xh in range(NXH)]


def along_y(z, xl, xh, c):
    return [device(z, xl, y, xh, c) for y in range(NY)]


def x_groups(c):
    return [along_x(z, y, c) for z in range(NZ) for y in range(NY)]


def y_groups(c):
    return [along_y(z, xl, xh, c) for z in range(NZ) for xl in range(NXL) for xh in range(NXH)]


SITES = [(xl, y, xh) for xl in range(NXL) for y in range(NY) for xh in range(NXH)]
ORDER = [(z + NZ // 2) % NZ for z in range(NZ)]
COLUMN_GROUPS = [[device(z, *s, c) for z in ORDER for c in range(NC)] for s in SITES]
Z_GROUPS = [[device(z, *s, c) for z in ORDER] for s in SITES for c in range(NC)]
FIRST_GROUPS = x_groups(0) + y_groups(1)
SECOND_GROUPS = y_groups(0) + x_groups(1)
PLANE_GROUPS = [[device(z, *s, c) for s in SITES] for z in range(NZ) for c in range(NC)]
LAST = [(xl, (y + NY // 2) % NY, 1 - xh) for xl, y, xh in SITES]
LAYER_GROUPS = [[device(z, *s, c) for s in LAST for c in range(NC)] for z in range(NZ)]
PAIRS = [[2 * i, 2 * i + 1] for i in range(NZ * PLANE)]
SWAP = [(i, i ^ 1) for i in range(NZ * PLANE * NC)]


def ring(shift):
    pairs = []
    for z in range(NZ):
        for xl, y, xh in SITES:
            pairs.append((device(z, xl, y, xh, 0), device(z, xl, (y + shift) % NY, xh, 0)))
            x = (xh * NXL + xl + shift) % NX
            pairs.append((device(z, xl, y, xh, 1), device(z, x % NXL, y, x // NXL, 1)))
    return pairs


def exchange(blocks, groups):
    return lax.all_to_all(blocks, BOTH, 0, 0, axis_index_groups=groups)


def spread(block, groups):
    number = len(groups[0])
    return exchange(jnp.broadcast_to(block[None], (number,) + block.shape), groups)


def columns(a, b):
    return lax.dot_general(a, b, (((1,), (0,)), ((), ())), preferred_element_type=jnp.float32)


SHIFTS = (0, 2, 1, 3)
ROWS = 192
ALL_ROWS = 2 * ROWS + 2 * 64
GROUPS = 4
SLABS = NZ // GROUPS


def block_kernel(dest_ref, *refs):
    lines = refs[0:4]
    w_ref, f_ref, h_ref, x_ref, acc_ref, s_ref = refs[4:]
    lane16 = lax.broadcasted_iota(jnp.int32, (16, 128), 1)
    first = (lane16 < 64).astype(jnp.float32).astype(jnp.bfloat16)
    second = (lane16 >= 64).astype(jnp.float32).astype(jnp.bfloat16)
    for group in range(GROUPS):
        for k in range(4):
            for j in range(4):
                place = dest_ref[k * 4 + j]
                for z in range(group * SLABS, group * SLABS + SLABS):
                    slab = ORDER.index(z)
                    base = pl.multiple_of(z * 512 + place, 32)
                    x_ref[pl.ds(base, 32), 0:128] = lines[k][j, slab * 32 : slab * 32 + 32, :]
                    tile = lines[k][j, 512 + slab * 16 : 528 + slab * 16, :]
                    x_ref[pl.ds(base, 16), 128:256] = tile * first
                    x_ref[pl.ds(pl.multiple_of(base + 16, 16), 16), 128:256] = tile * second
        span = slice(group * SLABS * 512, (group + 1) * SLABS * 512)
        product = columns(w_ref[:, span], x_ref[span, :])
        if group == 0:
            acc_ref[...] = product
        else:
            acc_ref[...] += product

    def rows(start, size, lanes):
        return acc_ref[start : start + size, lanes * 128 : lanes * 128 + 128]

    def both(start):
        return jnp.concatenate([rows(start, 56, 0), rows(start + 192, 56, 0)], axis=0)

    def grads(ranges):
        low = jnp.concatenate([rows(*r, 0) for r in ranges], axis=0)
        high = jnp.concatenate([rows(*r, 1) for r in ranges], axis=0)
        lane = lax.broadcasted_iota(jnp.int32, low.shape, 1)
        return jnp.where(lane < 64, pltpu.roll(low, 32, 1), high + pltpu.roll(high, 64, 1))

    gate_sum, up_sum = both(0), both(64)
    hidden_grad = grads([(128, 56), (320, 56)])
    sigmoid_gate = jax.nn.sigmoid(gate_sum)
    silu_gate = gate_sum * sigmoid_gate
    hidden = (silu_gate * up_sum).astype(jnp.bfloat16)
    gate_grad = (
        hidden_grad * up_sum * sigmoid_gate * (1.0 + gate_sum * (1.0 - sigmoid_gate))
    ).astype(jnp.bfloat16)
    up_grad = (hidden_grad * silu_gate).astype(jnp.bfloat16)
    for n, factor in enumerate((gate_grad, up_grad, hidden)):
        start = n * 64 + 56
        projection = jnp.concatenate(
            [
                w_ref[base + start : base + start + 8, m * 128 : m * 128 + 64].astype(jnp.float32)
                for base in (0, ROWS)
                for m in range(7)
            ],
            axis=0,
        ).astype(jnp.bfloat16)
        s_ref[n * 64 : n * 64 + 64] = lax.dot_general(
            projection,
            factor,
            (((0,), (0,)), ((), ())),
            preferred_element_type=jnp.float32,
        )
    for p in range(PLANE):
        for r in range(3):
            f_ref[p, r] = s_ref[p * 12 + r * 4 : p * 12 + r * 4 + 4, :]
    h_ref[0:64] = rows(384, 64, 0)
    h_ref[64:128] = grads([(448, 64)])


def block(dest, lines, weights):
    inside = pl.BlockSpec(memory_space=pltpu.VMEM)
    return pl.pallas_call(
        block_kernel,
        in_specs=[pl.BlockSpec(memory_space=pltpu.SMEM)] + [inside] * 5,
        out_specs=[inside] * 2,
        out_shape=[
            jax.ShapeDtypeStruct((PLANE, 3, 4, 128), jnp.float32),
            jax.ShapeDtypeStruct((128, 128), jnp.float32),
        ],
        scratch_shapes=[
            pltpu.VMEM((8192, 256), jnp.bfloat16),
            pltpu.VMEM((ALL_ROWS, 256), jnp.float32),
            pltpu.VMEM((192, 128), jnp.float32),
        ],
        compiler_params=pltpu.CompilerParams(vmem_limit_bytes=24 * MIB),
        cost_estimate=pl.CostEstimate(
            flops=2 * ALL_ROWS * 8192 * 256, bytes_accessed=12 * MIB, transcendentals=112 * 128
        ),
    )(dest, *lines, weights)


def load_kernel(*refs):
    parts, w_ref, sems = refs[0:8], *refs[9:]
    copies = []
    for n, part in enumerate(parts):
        copies.append(pltpu.make_async_copy(part, w_ref.at[pl.ds(n * 64, 64)], sems.at[n]))
    for copy in copies:
        copy.start()
    for copy in copies:
        copy.wait()


def load(parts, after):
    return pl.pallas_call(
        load_kernel,
        in_specs=[pl.BlockSpec(memory_space=pl.ANY)] * 9,
        out_specs=pl.BlockSpec(memory_space=pltpu.VMEM),
        out_shape=pltpu.VMEM((ALL_ROWS, 8192), jnp.bfloat16),
        scratch_shapes=[pltpu.SemaphoreType.DMA((8,))],
        compiler_params=pltpu.CompilerParams(vmem_limit_bytes=16 * MIB),
        cost_estimate=pl.CostEstimate(flops=0, bytes_accessed=16 * MIB, transcendentals=0),
    )(*[pltpu.with_memory_space_constraint(part, pltpu.HBM) for part in parts], after)


def stack_kernel(*refs):
    weights, projections, outs = refs[0:3], refs[3:6], refs[6:9]
    for weight, out in zip(weights, outs):
        out[0:56, :] = weight[...]
        out[56:64, :] = jnp.zeros((8, out.shape[1]), jnp.bfloat16)

    @pl.when(pl.program_id(0) == 0)
    def _():
        for projection, out in zip(projections, outs):
            for m in range(7):
                out[56:64, m * 128 : m * 128 + 64] = projection[m * 8 : m * 8 + 8, :]


def stack(weights, projections):
    width = 2048
    weight = pl.BlockSpec((56, width), lambda s: (0, s))
    projection = pl.BlockSpec((56, 64), lambda s: (0, 0))
    return pl.pallas_call(
        stack_kernel,
        grid=(8192 // width,),
        in_specs=[weight] * 3 + [projection] * 3,
        out_specs=[pl.BlockSpec((64, width), lambda s: (0, s))] * 3,
        out_shape=[jax.ShapeDtypeStruct((64, 8192), jnp.bfloat16)] * 3,
        cost_estimate=pl.CostEstimate(flops=0, bytes_accessed=6 * MIB, transcendentals=0),
    )(*weights, *projections)


def unpack_kernel(column_ref, out_ref):
    left = lax.broadcasted_iota(jnp.int32, (8, 128), 1) < 64
    for z in range(NZ):
        halves = []
        for c in range(NC):
            place = z * NC + c
            wide = column_ref[place, 0:16, :]
            halves.append(column_ref[place, 16:24, :].astype(jnp.float32))
            for n in range(4):
                out_ref[n, place * 16 : place * 16 + 16, :] = wide
        top = jnp.where(left, halves[0], pltpu.roll(halves[1], 64, 1))
        low = jnp.where(left, pltpu.roll(halves[0], 64, 1), halves[1])
        rest = jnp.concatenate([top, low], axis=0).astype(jnp.bfloat16)
        for n in range(4):
            out_ref[n, 512 + z * 16 : 528 + z * 16, :] = rest


def unpack(column):
    inside = pl.BlockSpec(memory_space=pltpu.VMEM)
    return pl.pallas_call(
        unpack_kernel,
        in_specs=[inside],
        out_specs=inside,
        out_shape=jax.ShapeDtypeStruct((4, 768, 128), jnp.bfloat16),
        cost_estimate=pl.CostEstimate(flops=0, bytes_accessed=MIB, transcendentals=0),
    )(pltpu.with_memory_space_constraint(column, pltpu.VMEM))


def pack_kernel(t_ref, g_ref, out_ref):
    t, g = t_ref[...].astype(jnp.float32), g_ref[...].astype(jnp.float32)
    for c in range(NC):
        start = c * HALF
        mine = jnp.concatenate([g[:, start : start + LOW], t[:, start : start + HALF]], axis=1)
        rest = g[:, start + LOW : start + HALF]
        rest = jnp.concatenate([rest[0:8], rest[8:16]], axis=1)
        packed = jnp.concatenate([mine, rest], axis=0).astype(jnp.bfloat16)
        for z in range(NZ):
            out_ref[z * NC + c] = packed


def pack(tokens, out_grad):
    return pl.pallas_call(
        pack_kernel,
        out_shape=jax.ShapeDtypeStruct((NZ * NC, 24, 128), jnp.bfloat16),
        cost_estimate=pl.CostEstimate(flops=0, bytes_accessed=1 << 18, transcendentals=0),
    )(tokens, out_grad)


def outer_kernel(f_ref, h_ref, ids_ref, out_ref, s_ref):
    for p in range(PLANE):
        for c in range(NC):
            for r in range(3):
                row = p * 12 + r * 4
                s_ref[row : row + 4, c * 128 : c * 128 + 128] = f_ref[LAST.index(SITES[p]), c, r]
    known = jnp.concatenate([h_ref[0], h_ref[1]], axis=1)
    doc = lax.broadcasted_iota(jnp.int32, (DOCS, NC * 128), 0)
    inside = (ids_ref[...] == doc)[None]
    sides = (
        (s_ref[0:64, :], known[0:64]),
        (s_ref[64:128, :], known[0:64]),
        (known[64:128], s_ref[128:192, :]),
    )
    def parts(side):
        high = side.astype(jnp.bfloat16).astype(jnp.float32)
        return high, side - high

    for k, (left, right) in enumerate(sides):
        left_high, left_low = [
            jnp.where(inside, part[:, None, :], 0.0)
            .reshape(64 * DOCS, NC * 128)
            .astype(jnp.bfloat16)
            for part in parts(left)
        ]
        right_high, right_low = [part.astype(jnp.bfloat16) for part in parts(right)]
        blocks = lax.dot_general(
            jnp.concatenate([left_high, left_high, left_low], axis=1),
            jnp.concatenate([right_high, right_low, right_high], axis=1),
            (((1,), (1,)), ((), ())),
            preferred_element_type=jnp.float32,
        )
        for i in range(0, 64, 2):
            pair = [blocks[(i + n) * DOCS : (i + n + 1) * DOCS] for n in range(2)]
            out_ref[k, :, i * 64 : i * 64 + 128] = jnp.concatenate(pair, axis=1)


def outer(factors, known, ids):
    return pl.pallas_call(
        outer_kernel,
        out_shape=jax.ShapeDtypeStruct((3, DOCS, 4096), jnp.float32),
        scratch_shapes=[pltpu.VMEM((192, 256), jnp.float32)],
        compiler_params=pltpu.CompilerParams(vmem_limit_bytes=16 * MIB),
        cost_estimate=pl.CostEstimate(
            flops=2 * 3 * 512 * 256 * 64 * 3, bytes_accessed=2 * MIB, transcendentals=0
        ),
    )(factors, known, ids)


def local(
    tokens,
    out_grad,
    gate_weight,
    up_weight,
    down_weight,
    input_proj,
    output_proj,
    gate_proj,
    up_proj,
    hidden_proj,
    doc_ids,
):
    me = lax.axis_index("dp") * 16 + lax.axis_index("mp")
    core, x, y = me % NC, me // 2 % NXH * NXL + me // 16 % NXL, me // 4 % NY
    column = exchange(pack(tokens.T, out_grad.T), COLUMN_GROUPS)
    own = stack((gate_weight, up_weight, down_weight), (gate_proj, up_proj, hidden_proj))
    other = [lax.ppermute(part, BOTH, SWAP) for part in own]
    line = exchange(unpack(column), FIRST_GROUPS)
    line, *other = lax.optimization_barrier((line, *other))
    lines = [line] + [lax.ppermute(line, BOTH, ring(shift)) for shift in SHIFTS[1:]]
    dest = []
    for shift in SHIFTS:
        from_y, from_x = (y - shift) % NY, (x - shift) % NX
        for j in range(4):
            even = j // NXH * 8 + from_y * 2 + j % NXH
            odd = from_x % NXL * 8 + j * 2 + from_x // NXL
            dest.append(jnp.where(core == 0, even, odd) * 32)
    dest = jnp.stack(dest).astype(jnp.int32)

    weights = load((*own, *other, input_proj, output_proj), line)
    factors, known = block(dest, lines, weights)
    known = lax.all_gather(known, BOTH, axis=0, axis_index_groups=PAIRS)
    part = exchange(factors, PLANE_GROUPS).sum(0)
    part = spread(part, Z_GROUPS).sum(0)
    factors = spread(part, LAYER_GROUPS).reshape(PLANE, NC, 3, 4, 128)
    ids = jnp.pad(doc_ids.reshape(NC, HALF), ((0, 0), (LOW, 0)), constant_values=-1)
    return outer(factors, known, ids.reshape(1, NC * 128))


def solution(mesh):
    return jax.shard_map(
        local,
        mesh=mesh,
        in_specs=(
            P(None, BOTH),
            P(None, BOTH),
            P(BOTH, None),
            P(BOTH, None),
            P(BOTH, None),
            P(),
            P(),
            P(BOTH, None),
            P(BOTH, None),
            P(BOTH, None),
            P(),
        ),
        out_specs=P(),
        check_vma=False,
    )
```

```python
import jax
import jax.numpy as jnp
from jax import lax
from jax.experimental import pallas as pl
from jax.experimental.pallas import tpu as pltpu
from jax.sharding import PartitionSpec as P

DOCS = 8
BOTH = ("dp", "mp")
NZ, NXL, NY, NXH, NC = 16, 2, 4, 2, 2
NX = NXL * NXH
PLANE = NX * NY
LOW = 32
HALF = 96
MIB = 1 << 20


def device(z, xl, y, xh, c):
    return (((z * NXL + xl) * NY + y) * NXH + xh) * NC + c


def along_x(z, y, c):
    return [device(z, xl, y, xh, c) for xl in range(NXL) for xh in range(NXH)]


def along_y(z, xl, xh, c):
    return [device(z, xl, y, xh, c) for y in range(NY)]


def x_groups(c):
    return [along_x(z, y, c) for z in range(NZ) for y in range(NY)]


def y_groups(c):
    return [along_y(z, xl, xh, c) for z in range(NZ) for xl in range(NXL) for xh in range(NXH)]


SITES = [(xl, y, xh) for xl in range(NXL) for y in range(NY) for xh in range(NXH)]
ORDER = [(z + NZ // 2) % NZ for z in range(NZ)]
COLUMN_GROUPS = [[device(z, *s, c) for z in ORDER for c in range(NC)] for s in SITES]
Z_GROUPS = [[device(z, *s, c) for z in ORDER] for s in SITES for c in range(NC)]
FIRST_GROUPS = x_groups(0) + y_groups(1)
SECOND_GROUPS = y_groups(0) + x_groups(1)
LAST = [(xl, (y + NY // 2) % NY, 1 - xh) for xl, y, xh in SITES]
PLANE_GROUPS = [[device(z, *s, c) for s in LAST] for z in range(NZ) for c in range(NC)]
LAYER_GROUPS = [[device(z, *s, c) for s in LAST for c in range(NC)] for z in range(NZ)]
PAIRS = [[2 * i, 2 * i + 1] for i in range(NZ * PLANE)]
SWAP = [(i, i ^ 1) for i in range(NZ * PLANE * NC)]


def ring(shift):
    pairs = []
    for z in range(NZ):
        for xl, y, xh in SITES:
            pairs.append((device(z, xl, y, xh, 0), device(z, xl, (y + shift) % NY, xh, 0)))
            x = (xh * NXL + xl + shift) % NX
            pairs.append((device(z, xl, y, xh, 1), device(z, x % NXL, y, x // NXL, 1)))
    return pairs


def exchange(blocks, groups):
    return lax.all_to_all(blocks, BOTH, 0, 0, axis_index_groups=groups)


def spread(block, groups):
    number = len(groups[0])
    return exchange(jnp.broadcast_to(block[None], (number,) + block.shape), groups)


def columns(a, b):
    return lax.dot_general(a, b, (((1,), (0,)), ((), ())), preferred_element_type=jnp.float32)


SHIFTS = (0, 2, 1, 3)
ROWS = 192
ALL_ROWS = 2 * ROWS + 2 * 64
GROUPS = 4
SLABS = NZ // GROUPS


def block_kernel(dest_ref, *refs):
    lines = refs[0:4]
    w_ref, f_ref, h_ref, x_ref, acc_ref, s_ref = refs[4:]
    lane16 = lax.broadcasted_iota(jnp.int32, (16, 128), 1)
    first = (lane16 < 64).astype(jnp.float32).astype(jnp.bfloat16)
    second = (lane16 >= 64).astype(jnp.float32).astype(jnp.bfloat16)
    for group in range(GROUPS):
        for k in range(4):
            for j in range(4):
                place = dest_ref[k * 4 + j]
                for z in range(group * SLABS, group * SLABS + SLABS):
                    slab = ORDER.index(z)
                    base = pl.multiple_of(z * 512 + place, 32)
                    x_ref[pl.ds(base, 32), 0:128] = lines[k][j, slab * 32 : slab * 32 + 32, :]
                    tile = lines[k][j, 512 + slab * 16 : 528 + slab * 16, :]
                    x_ref[pl.ds(base, 16), 128:256] = tile * first
                    x_ref[pl.ds(pl.multiple_of(base + 16, 16), 16), 128:256] = tile * second
        span = slice(group * SLABS * 512, (group + 1) * SLABS * 512)
        product = columns(w_ref[:, span], x_ref[span, :])
        if group == 0:
            acc_ref[...] = product
        else:
            acc_ref[...] += product

    def rows(start, size, lanes):
        return acc_ref[start : start + size, lanes * 128 : lanes * 128 + 128]

    def both(start):
        return jnp.concatenate([rows(start, 56, 0), rows(start + 192, 56, 0)], axis=0)

    def grads(ranges):
        low = jnp.concatenate([rows(*r, 0) for r in ranges], axis=0)
        high = jnp.concatenate([rows(*r, 1) for r in ranges], axis=0)
        lane = lax.broadcasted_iota(jnp.int32, low.shape, 1)
        return jnp.where(lane < 64, pltpu.roll(low, 32, 1), high + pltpu.roll(high, 64, 1))

    gate_sum, up_sum = both(0), both(64)
    hidden_grad = grads([(128, 56), (320, 56)])
    sigmoid_gate = jax.nn.sigmoid(gate_sum)
    silu_gate = gate_sum * sigmoid_gate
    hidden = (silu_gate * up_sum).astype(jnp.bfloat16)
    gate_grad = (
        hidden_grad * up_sum * sigmoid_gate * (1.0 + gate_sum * (1.0 - sigmoid_gate))
    ).astype(jnp.bfloat16)
    up_grad = (hidden_grad * silu_gate).astype(jnp.bfloat16)
    for n, factor in enumerate((gate_grad, up_grad, hidden)):
        start = n * 64 + 56
        projection = jnp.concatenate(
            [
                w_ref[base + start : base + start + 8, m * 128 : m * 128 + 64].astype(jnp.float32)
                for base in (0, ROWS)
                for m in range(7)
            ],
            axis=0,
        ).astype(jnp.bfloat16)
        s_ref[n * 64 : n * 64 + 64] = lax.dot_general(
            projection,
            factor,
            (((0,), (0,)), ((), ())),
            preferred_element_type=jnp.float32,
        )
    for p in range(PLANE):
        for r in range(3):
            f_ref[p, r] = s_ref[p * 12 + r * 4 : p * 12 + r * 4 + 4, :]
    h_ref[0:64] = rows(384, 64, 0)
    h_ref[64:128] = grads([(448, 64)])


def block(dest, lines, weights):
    inside = pl.BlockSpec(memory_space=pltpu.VMEM)
    return pl.pallas_call(
        block_kernel,
        in_specs=[pl.BlockSpec(memory_space=pltpu.SMEM)] + [inside] * 5,
        out_specs=[inside] * 2,
        out_shape=[
            jax.ShapeDtypeStruct((PLANE, 3, 4, 128), jnp.float32),
            jax.ShapeDtypeStruct((128, 128), jnp.float32),
        ],
        scratch_shapes=[
            pltpu.VMEM((8192, 256), jnp.bfloat16),
            pltpu.VMEM((ALL_ROWS, 256), jnp.float32),
            pltpu.VMEM((192, 128), jnp.float32),
        ],
        compiler_params=pltpu.CompilerParams(vmem_limit_bytes=24 * MIB),
        cost_estimate=pl.CostEstimate(
            flops=2 * ALL_ROWS * 8192 * 256, bytes_accessed=12 * MIB, transcendentals=112 * 128
        ),
    )(dest, *lines, weights)


def load_kernel(*refs):
    parts, w_ref, sems = refs[0:8], *refs[9:]
    copies = []
    for n, part in enumerate(parts):
        copies.append(pltpu.make_async_copy(part, w_ref.at[pl.ds(n * 64, 64)], sems.at[n]))
    for copy in copies:
        copy.start()
    for copy in copies:
        copy.wait()


def load(parts, after):
    return pl.pallas_call(
        load_kernel,
        in_specs=[pl.BlockSpec(memory_space=pl.ANY)] * 9,
        out_specs=pl.BlockSpec(memory_space=pltpu.VMEM),
        out_shape=pltpu.VMEM((ALL_ROWS, 8192), jnp.bfloat16),
        scratch_shapes=[pltpu.SemaphoreType.DMA((8,))],
        compiler_params=pltpu.CompilerParams(vmem_limit_bytes=16 * MIB),
        cost_estimate=pl.CostEstimate(flops=0, bytes_accessed=16 * MIB, transcendentals=0),
    )(*[pltpu.with_memory_space_constraint(part, pltpu.HBM) for part in parts], after)


def stack_kernel(*refs):
    weights, projections, outs = refs[0:3], refs[3:6], refs[6:9]
    for weight, out in zip(weights, outs):
        out[0:56, :] = weight[...]
        out[56:64, :] = jnp.zeros((8, out.shape[1]), jnp.bfloat16)

    @pl.when(pl.program_id(0) == 0)
    def _():
        for projection, out in zip(projections, outs):
            for m in range(7):
                out[56:64, m * 128 : m * 128 + 64] = projection[m * 8 : m * 8 + 8, :]


def stack(weights, projections):
    width = 2048
    weight = pl.BlockSpec((56, width), lambda s: (0, s))
    projection = pl.BlockSpec((56, 64), lambda s: (0, 0))
    return pl.pallas_call(
        stack_kernel,
        grid=(8192 // width,),
        in_specs=[weight] * 3 + [projection] * 3,
        out_specs=[pl.BlockSpec((64, width), lambda s: (0, s))] * 3,
        out_shape=[jax.ShapeDtypeStruct((64, 8192), jnp.bfloat16)] * 3,
        cost_estimate=pl.CostEstimate(flops=0, bytes_accessed=6 * MIB, transcendentals=0),
    )(*weights, *projections)


def unpack_kernel(column_ref, out_ref):
    left = lax.broadcasted_iota(jnp.int32, (8, 128), 1) < 64
    for z in range(NZ):
        halves = []
        for c in range(NC):
            place = z * NC + c
            wide = column_ref[place, 0:16, :]
            halves.append(column_ref[place, 16:24, :].astype(jnp.float32))
            for n in range(4):
                out_ref[n, place * 16 : place * 16 + 16, :] = wide
        top = jnp.where(left, halves[0], pltpu.roll(halves[1], 64, 1))
        low = jnp.where(left, pltpu.roll(halves[0], 64, 1), halves[1])
        rest = jnp.concatenate([top, low], axis=0).astype(jnp.bfloat16)
        for n in range(4):
            out_ref[n, 512 + z * 16 : 528 + z * 16, :] = rest


def unpack(column):
    inside = pl.BlockSpec(memory_space=pltpu.VMEM)
    return pl.pallas_call(
        unpack_kernel,
        in_specs=[inside],
        out_specs=inside,
        out_shape=jax.ShapeDtypeStruct((4, 768, 128), jnp.bfloat16),
        cost_estimate=pl.CostEstimate(flops=0, bytes_accessed=MIB, transcendentals=0),
    )(pltpu.with_memory_space_constraint(column, pltpu.VMEM))


def pack_kernel(t_ref, g_ref, out_ref):
    t, g = t_ref[...].astype(jnp.float32), g_ref[...].astype(jnp.float32)
    for c in range(NC):
        start = c * HALF
        mine = jnp.concatenate([g[:, start : start + LOW], t[:, start : start + HALF]], axis=1)
        rest = g[:, start + LOW : start + HALF]
        rest = jnp.concatenate([rest[0:8], rest[8:16]], axis=1)
        packed = jnp.concatenate([mine, rest], axis=0).astype(jnp.bfloat16)
        for z in range(NZ):
            out_ref[z * NC + c] = packed


def pack(tokens, out_grad):
    return pl.pallas_call(
        pack_kernel,
        out_shape=jax.ShapeDtypeStruct((NZ * NC, 24, 128), jnp.bfloat16),
        cost_estimate=pl.CostEstimate(flops=0, bytes_accessed=1 << 18, transcendentals=0),
    )(tokens, out_grad)


def outer_kernel(f_ref, h_ref, ids_ref, out_ref, s_ref):
    for p in range(PLANE):
        for c in range(NC):
            for r in range(3):
                row = p * 12 + r * 4
                s_ref[row : row + 4, c * 128 : c * 128 + 128] = f_ref[p, c, r]
    known = jnp.concatenate([h_ref[0], h_ref[1]], axis=1)
    doc = lax.broadcasted_iota(jnp.int32, (DOCS, NC * 128), 0)
    inside = (ids_ref[...] == doc)[None]
    sides = (
        (s_ref[0:64, :], known[0:64]),
        (s_ref[64:128, :], known[0:64]),
        (known[64:128], s_ref[128:192, :]),
    )
    def parts(side):
        high = side.astype(jnp.bfloat16).astype(jnp.float32)
        return high, side - high

    for k, (left, right) in enumerate(sides):
        left_high, left_low = [
            jnp.where(inside, part[:, None, :], 0.0)
            .reshape(64 * DOCS, NC * 128)
            .astype(jnp.bfloat16)
            for part in parts(left)
        ]
        right_high, right_low = [part.astype(jnp.bfloat16) for part in parts(right)]
        blocks = lax.dot_general(
            jnp.concatenate([left_high, left_high, left_low], axis=1),
            jnp.concatenate([right_high, right_low, right_high], axis=1),
            (((1,), (1,)), ((), ())),
            preferred_element_type=jnp.float32,
        )
        for i in range(0, 64, 2):
            pair = [blocks[(i + n) * DOCS : (i + n + 1) * DOCS] for n in range(2)]
            out_ref[k, :, i * 64 : i * 64 + 128] = jnp.concatenate(pair, axis=1)


def outer(factors, known, ids):
    return pl.pallas_call(
        outer_kernel,
        out_shape=jax.ShapeDtypeStruct((3, DOCS, 4096), jnp.float32),
        scratch_shapes=[pltpu.VMEM((192, 256), jnp.float32)],
        compiler_params=pltpu.CompilerParams(vmem_limit_bytes=16 * MIB),
        cost_estimate=pl.CostEstimate(
            flops=2 * 3 * 512 * 256 * 64 * 3, bytes_accessed=2 * MIB, transcendentals=0
        ),
    )(factors, known, ids)


def local(
    tokens,
    out_grad,
    gate_weight,
    up_weight,
    down_weight,
    input_proj,
    output_proj,
    gate_proj,
    up_proj,
    hidden_proj,
    doc_ids,
):
    me = lax.axis_index("dp") * 16 + lax.axis_index("mp")
    core, x, y = me % NC, me // 2 % NXH * NXL + me // 16 % NXL, me // 4 % NY
    column = exchange(pack(tokens.T, out_grad.T), COLUMN_GROUPS)
    own = stack((gate_weight, up_weight, down_weight), (gate_proj, up_proj, hidden_proj))
    other = [lax.ppermute(part, BOTH, SWAP) for part in own]
    line = exchange(unpack(column), FIRST_GROUPS)
    line, *other = lax.optimization_barrier((line, *other))
    lines = [line] + [lax.ppermute(line, BOTH, ring(shift)) for shift in SHIFTS[1:]]
    dest = []
    for shift in SHIFTS:
        from_y, from_x = (y - shift) % NY, (x - shift) % NX
        for j in range(4):
            even = j // NXH * 8 + from_y * 2 + j % NXH
            odd = from_x % NXL * 8 + j * 2 + from_x // NXL
            dest.append(jnp.where(core == 0, even, odd) * 32)
    dest = jnp.stack(dest).astype(jnp.int32)

    weights = load((*own, *other, input_proj, output_proj), line)
    factors, known = block(dest, lines, weights)
    known = lax.all_gather(known, BOTH, axis=0, axis_index_groups=PAIRS)
    part = exchange(factors, PLANE_GROUPS).sum(0)
    part = spread(part, Z_GROUPS).sum(0)
    factors = spread(part, LAYER_GROUPS).reshape(PLANE, NC, 3, 4, 128)
    ids = jnp.pad(doc_ids.reshape(NC, HALF), ((0, 0), (LOW, 0)), constant_values=-1)
    return outer(factors, known, ids.reshape(1, NC * 128))


def solution(mesh):
    return jax.shard_map(
        local,
        mesh=mesh,
        in_specs=(
            P(None, BOTH),
            P(None, BOTH),
            P(BOTH, None),
            P(BOTH, None),
            P(BOTH, None),
            P(),
            P(),
            P(BOTH, None),
            P(BOTH, None),
            P(BOTH, None),
            P(),
        ),
        out_specs=P(),
        check_vma=False,
    )
```
